32 devices in a mesh: dp: 8 (over z, x), fsdp: 4 (over y, core).
Axes of the slice: x: 2, y: 2, z: 4, core: 2. Of those that a mesh axis runs over, the one named last changes fastest.
Arguments:
- inputs: bfloat16 [128, 14, 14, 256], P(('dp', 'fsdp')), may hold values from -6 to 6
- out_grads: bfloat16 [128, 14, 14, 256], P(('dp', 'fsdp')), may hold values from -6 to 6
- patch_basis: bfloat16 [1152, 2304], P(None, 'fsdp'), may hold values from -0.1875 to 0.1875
- output_basis: bfloat16 [256, 256], P(None, 'fsdp'), may hold values from -0.375 to 0.375
Outputs:
- second_moment: float32 [256, 2304], P('dp', 'fsdp')
- scaled_sum: float32 [256, 2304], P('dp', 'fsdp')
The draws below stay inside these ranges and needn't reach their ends.
All inputs are finite; a program needn't handle non-finite values.
Results may differ from the reference program's by a relative error of at most 0.0041.
Values may be sent and summed in bfloat16 or wider, within the bound.
A program may use at most 64 MiB of HBM per device.

```python
import math
import jax
import jax.numpy as jnp
from jax import lax

C = 256
OUTC = 256
SIDE = 14
P_SIZE = 2304
HALF = 1152
EXAMPLES = 128


def steps_of(key, shape, split, least, high):
    level = 1.0
    for axis_at, blocks in split:
        steps = jax.random.uniform(jax.random.fold_in(jax.random.fold_in(key, 6), axis_at), (blocks,), jnp.float32, least / len(split), high / len(split))
        level = level * jnp.repeat(jnp.exp(steps), shape[axis_at] // blocks).reshape((-1,) + (1,) * (len(shape) - 1 - axis_at))
    return level


def gaussian(own_key, shape, scale, reach, shards=(), held_as=jnp.bfloat16):
    values = scale * jax.random.normal(own_key, shape, jnp.float32)
    if shards:
        values = values * steps_of(own_key, shape, shards, -0.22, 0.18)
    return jnp.clip(values, -reach, reach).astype(held_as)


def setup_inputs(seed: int = 0) -> dict:
    key_of = jax.random.split(jax.random.key(seed), 5)
    inputs = gaussian(key_of[0], (EXAMPLES, SIDE, SIDE, C), 1.0, 6.0, ((0, 32),))
    out_grads = gaussian(key_of[1], (EXAMPLES, SIDE, SIDE, OUTC), 1.0, 6.0, ((0, 32),))
    patch_basis = gaussian(key_of[2], (HALF, P_SIZE), HALF ** -0.5, 0.1875, ((1, 4),))
    output_basis = gaussian(key_of[3], (OUTC, OUTC), OUTC ** -0.5, 0.375, ((1, 4),))
    return {"inputs": inputs, "out_grads": out_grads, "patch_basis": patch_basis, "output_basis": output_basis}


def patch_rows(feature_maps):
    count = feature_maps.shape[0]
    grid_side = feature_maps.shape[1]
    padded = jnp.pad(feature_maps, ((0, 0), (1, 1), (1, 1), (0, 0)))
    shifted = [padded[:, row_tap:row_tap + grid_side, col_tap:col_tap + grid_side, :] for row_tap in range(3) for col_tap in range(3)]
    return jnp.concatenate(shifted, axis=3).reshape(count, grid_side * grid_side, -1)

def reference(inputs, out_grads, patch_basis, output_basis):
    block_width = patch_basis.shape[0]

    def accumulate(carried, sample):
        example_input, example_grad = sample
        patches = patch_rows(example_input[None])[0]
        low_part = jnp.dot(patches[:, :block_width], patch_basis[:, :block_width], preferred_element_type=jnp.float32)
        high_part = jnp.dot(patches[:, block_width:], patch_basis[:, block_width:], preferred_element_type=jnp.float32)
        rotated = jnp.concatenate([low_part, high_part], axis=1).astype(jnp.bfloat16)
        grad_rot = jnp.dot(example_grad.reshape(-1, OUTC), output_basis, preferred_element_type=jnp.float32).astype(jnp.bfloat16)
        projected = jnp.dot(grad_rot.T, rotated, preferred_element_type=jnp.float32) * (1.0 / SIDE)
        return ((carried[0] + projected * projected, carried[1] + projected), None)
    empty_sums = jnp.zeros((OUTC, 9 * C), jnp.float32)
    (squares, linear), unused = lax.scan(accumulate, (empty_sums, empty_sums), (inputs, out_grads))
    return (squares / EXAMPLES, linear * (1.0 / math.sqrt(EXAMPLES)))
```

```python
import functools
import math

import jax
import jax.numpy as jnp
from jax import lax
from jax.experimental import pallas as pl
from jax.experimental.pallas import tpu as pltpu
from jax.sharding import PartitionSpec as P

MESH = pl.DeviceIdType.MESH
HALVES = 2
PADDED = 16
LANES = 128


def kernel(
    nd, nf, examples, x_ref, g_ref, pb_ref, ob_ref, sq_out, ln_out,
    xbuf, gstage, obbuf, rot, gr, taps, shifts, sq, ln, rs_send, rs_recv,
    ob_snd, ob_rcv, x_snd, x_rcv, g_snd, g_rcv, r_snd, r_rcv,
):
    d = lax.axis_index("dp")
    f = lax.axis_index("fsdp")
    nh = nf // 2
    h, c = f // 2, f % 2
    sibling = 2 * h + 1 - c
    side = x_ref.shape[1]
    channels = x_ref.shape[3]
    height, cols = pb_ref.shape
    outc = ob_ref.shape[0]
    own_cols = ob_ref.shape[1]
    rows = side * PADDED
    flat = xbuf.shape[1] * PADDED
    quart = outc // HALVES
    per_dp = quart // nd
    total = nd * nf * examples
    f32, bf16 = jnp.float32, jnp.bfloat16

    barrier = pltpu.get_barrier_semaphore()
    pl.semaphore_signal(barrier, inc=1, device_id=(d, sibling), device_id_type=MESH)
    for j in range(1, nh):
        pl.semaphore_signal(
            barrier, inc=1, device_id=(d, 2 * ((h + j) % nh) + c), device_id_type=MESH
        )
    for j in range(1, nd):
        pl.semaphore_signal(barrier, inc=1, device_id=((d + j) % nd, f), device_id_type=MESH)

    def source(j, t):
        return 2 * ((h + j) % nh) + c + t * (1 - 2 * c)

    def clear(n, carry):
        xbuf[n, 0] = jnp.zeros((PADDED, channels), bf16)
        xbuf[n, pl.ds(side + 1, xbuf.shape[1] - side - 1)] = jnp.zeros(
            (xbuf.shape[1] - side - 1, PADDED, channels), bf16
        )
        return carry

    lax.fori_loop(0, nf * examples, clear, 0)

    def stage(e, carry):
        n = f * examples + e
        xbuf[n, pl.ds(1, side)] = jnp.zeros((side, PADDED, channels), bf16)
        xbuf[n, pl.ds(1, side), pl.ds(0, side), :] = x_ref[e]
        gstage[e] = jnp.zeros((side, PADDED, outc), bf16)
        gstage[e, :, pl.ds(0, side), :] = g_ref[e]
        return carry

    lax.fori_loop(0, examples, stage, 0)
    obbuf[f] = ob_ref[...]

    pl.semaphore_wait(barrier, nd - 1 + nh)

    def route(j, t):
        to = jnp.where(t == 1, sibling, 2 * ((h + j) % nh) + c)
        back = (nh - j) % nh if isinstance(j, int) else lax.rem(nh - j, nh)
        return (d, to), back

    def ob_copy(j, t, own):
        to, back = route(j, t)
        s = f if own else source(j, 0)
        slot = back if t == 0 else j
        return pltpu.make_async_remote_copy(
            src_ref=obbuf.at[s], dst_ref=obbuf.at[s], send_sem=ob_snd.at[j, t],
            recv_sem=ob_rcv.at[slot, t], device_id=to, device_id_type=MESH)

    def ob_arrival(j, t):
        s = source(j, t)
        return pltpu.make_async_remote_copy(
            src_ref=obbuf.at[s], dst_ref=obbuf.at[s], send_sem=ob_snd.at[j, t],
            recv_sem=ob_rcv.at[j, t], device_id=(d, sibling), device_id_type=MESH)

    def x_copy(j, t, e, own):
        to, back = route(j, t)
        s = f if own else source(j, 0)
        slot = back if t == 0 else j
        ref = xbuf.at[s * examples + e, pl.ds(1, side)]
        return pltpu.make_async_remote_copy(
            src_ref=ref, dst_ref=ref, send_sem=x_snd.at[j, t, e],
            recv_sem=x_rcv.at[slot, t, e], device_id=to, device_id_type=MESH)

    def x_arrival(j, t, e):
        ref = xbuf.at[source(j, t) * examples + e, pl.ds(1, side)]
        return pltpu.make_async_remote_copy(
            src_ref=ref, dst_ref=ref, send_sem=x_snd.at[j, t, e],
            recv_sem=x_rcv.at[j, t, e], device_id=(d, sibling), device_id_type=MESH)

    def g_copy(q, j, t, e, own):
        to, back = route(j, t)
        s = f if own else source(j, 0)
        slot = back if t == 0 else j
        ref = gr.at[q, s * examples + e]
        return pltpu.make_async_remote_copy(
            src_ref=ref, dst_ref=ref, send_sem=g_snd.at[q, j, t, e],
            recv_sem=g_rcv.at[q, slot, t, e], device_id=to, device_id_type=MESH)

    def g_arrival(q, j, t, e):
        ref = gr.at[q, source(j, t) * examples + e]
        return pltpu.make_async_remote_copy(
            src_ref=ref, dst_ref=ref, send_sem=g_snd.at[q, j, t, e],
            recv_sem=g_rcv.at[q, j, t, e], device_id=(d, sibling), device_id_type=MESH)

    def r_copy(q, j):
        return pltpu.make_async_remote_copy(
            src_ref=rs_send.at[q, j], dst_ref=rs_recv.at[q, j], send_sem=r_snd.at[q, j],
            recv_sem=r_rcv.at[q, j], device_id=((d + j) % nd, f), device_id_type=MESH)

    def each(count, body):
        def step(i, carry):
            body(i)
            return carry
        lax.fori_loop(0, count, step, 0)

    for j in range(1, nh):
        ob_copy(j, 0, True).start()
    ob_copy(0, 1, True).start()
    for j in range(1, nh):
        each(examples, lambda e: x_copy(j, 0, e, True).start())
    each(examples, lambda e: x_copy(0, 1, e, True).start())

    sq[...] = jnp.zeros_like(sq)
    ln[...] = jnp.zeros_like(ln)
    into = lax.broadcasted_iota(jnp.int32, (flat, flat), 0)
    out_of = lax.broadcasted_iota(jnp.int32, (flat, flat), 1)
    shifts[0] = (out_of == into - 1).astype(f32).astype(bf16)
    shifts[1] = (out_of == into + 1).astype(f32).astype(bf16)

    chunks = channels // LANES
    first = ((f * cols) // height) * (height // LANES)

    def rotate(n):
        plain = xbuf[n].reshape(flat, channels)
        before = jnp.dot(shifts[0], plain, preferred_element_type=f32).astype(bf16)
        after = jnp.dot(shifts[1], plain, preferred_element_type=f32).astype(bf16)
        for kx, value in enumerate((before, plain, after)):
            for k in range(chunks):
                taps[kx * chunks + k] = value[:, k * LANES : (k + 1) * LANES]
        pieces = []
        for i in range(height // LANES):
            at = first + i
            tap, k = at // chunks, at % chunks
            ky, kx = tap // 3, tap % 3
            start = pl.multiple_of(ky * PADDED, PADDED)
            pieces.append(taps[kx * chunks + k, pl.ds(start, rows), :])
        patches = jnp.concatenate(pieces, axis=1)
        rot[n] = jnp.dot(patches, pb_ref[...], preferred_element_type=f32).astype(bf16)

    def project(q, n):
        value = lax.dot_general(
            gr[q, n], rot[n], (((0,), (0,)), ((), ())), preferred_element_type=f32
        ) * (1.0 / side)
        sq[q] += value * value
        ln[q] += value

    each(examples, lambda e: rotate(f * examples + e))

    ob_arrival(0, 1).wait_recv()
    for j in range(1, nh):
        ob_arrival(j, 0).wait_recv()
        ob_copy(j, 1, False).start()
    for j in range(1, nh):
        ob_arrival(j, 1).wait_recv()
    column = lax.broadcasted_iota(jnp.int32, (own_cols, outc), 0)
    place = lax.broadcasted_iota(jnp.int32, (own_cols, outc), 1)
    half, rest = place // quart, place % quart
    wanted = (rest // per_dp) * (per_dp * HALVES) + half * per_dp + rest % per_dp
    basis = jnp.zeros((outc, outc), f32)
    for s in range(nf):
        pick = (column + s * own_cols == wanted).astype(f32).astype(bf16)
        basis = basis + jnp.dot(obbuf[s], pick, preferred_element_type=f32)
    basis = basis.astype(bf16)
    for e in range(examples):
        value = jnp.dot(
            gstage[e].reshape(rows, outc), basis, preferred_element_type=f32
        ).astype(bf16)
        for q in range(HALVES):
            gr[q, f * examples + e] = value[:, q * quart : (q + 1) * quart]
    for q in range(HALVES):
        for j in range(1, nh):
            each(examples, lambda e: g_copy(q, j, 0, e, True).start())
        each(examples, lambda e: g_copy(q, 0, 1, e, True).start())

    def own_project(e):
        for q in range(HALVES):
            project(q, f * examples + e)

    each(examples, own_project)

    def sibling_rotate(e):
        x_arrival(0, 1, e).wait_recv()
        rotate(sibling * examples + e)

    each(examples, sibling_rotate)

    def sibling_project(e):
        for q in range(HALVES):
            g_arrival(q, 0, 1, e).wait_recv()
            project(q, sibling * examples + e)

    each(examples, sibling_project)

    def far_rotate(i):
        j, e = 1 + i // examples, i % examples
        x_arrival(j, 0, e).wait_recv()
        x_copy(j, 1, e, False).start()
        rotate(source(j, 0) * examples + e)
        x_arrival(j, 1, e).wait_recv()
        rotate(source(j, 1) * examples + e)

    each((nh - 1) * examples, far_rotate)

    for q in range(HALVES):
        def far_project(i):
            j, e = 1 + i // examples, i % examples
            g_arrival(q, j, 0, e).wait_recv()
            g_copy(q, j, 1, e, False).start()
            project(q, source(j, 0) * examples + e)
            g_arrival(q, j, 1, e).wait_recv()
            project(q, source(j, 1) * examples + e)

        each((nh - 1) * examples, far_project)

        def hand_out(i):
            j = i + 1
            start = pl.multiple_of(((d + j) % nd) * per_dp, per_dp)
            both = jnp.concatenate(
                [sq[q, pl.ds(start, per_dp), :], ln[q, pl.ds(start, per_dp), :]], axis=0
            )
            rs_send[q, j] = both.astype(bf16)
            r_copy(q, j).start()

        each(nd - 1, hand_out)

    for q in range(HALVES):
        start = pl.multiple_of(d * per_dp, per_dp)
        total_sq = sq[q, pl.ds(start, per_dp), :]
        total_ln = ln[q, pl.ds(start, per_dp), :]
        for j in range(1, nd):
            r_copy(q, j).wait_recv()
            got = rs_recv[q, j].astype(f32)
            total_sq = total_sq + got[:per_dp]
            total_ln = total_ln + got[per_dp:]
        sq_out[pl.ds(q * per_dp, per_dp), :] = total_sq * (1.0 / total)
        ln_out[pl.ds(q * per_dp, per_dp), :] = total_ln * (1.0 / math.sqrt(total))

    ob_copy(0, 1, True).wait_send()
    each(examples, lambda e: x_copy(0, 1, e, True).wait_send())
    for q in range(HALVES):
        each(examples, lambda e: g_copy(q, 0, 1, e, True).wait_send())
        each(nd - 1, lambda i: r_copy(q, i + 1).wait_send())
    for j in range(1, nh):
        ob_copy(j, 0, True).wait_send()
        ob_copy(j, 1, False).wait_send()

        def sent(e):
            x_copy(j, 0, e, True).wait_send()
            x_copy(j, 1, e, False).wait_send()
            for q in range(HALVES):
                g_copy(q, j, 0, e, True).wait_send()
                g_copy(q, j, 1, e, False).wait_send()

        each(examples, sent)


def on_device(inputs, out_grads, patch_basis, output_basis):
    nd, nf = lax.axis_size("dp"), lax.axis_size("fsdp")
    nh = nf // 2
    examples, side, _, channels = inputs.shape
    cols = patch_basis.shape[1]
    outc, own_cols = output_basis.shape
    rows = side * PADDED
    quart = outc // HALVES
    per_dp = quart // nd
    held = nf * examples
    bf16, f32 = jnp.bfloat16, jnp.float32
    dma = pltpu.SemaphoreType.DMA
    vmem = pl.BlockSpec(memory_space=pltpu.VMEM)
    out = jax.ShapeDtypeStruct((outc // nd, cols), f32)
    return pl.pallas_call(
        functools.partial(kernel, nd, nf, examples),
        out_shape=(out, out),
        in_specs=[vmem] * 4,
        out_specs=(vmem, vmem),
        scratch_shapes=[
            pltpu.VMEM((held, side + 2, PADDED, channels), bf16),
            pltpu.VMEM((examples, side, PADDED, outc), bf16),
            pltpu.VMEM((nf, outc, own_cols), bf16),
            pltpu.VMEM((held, rows, cols), bf16),
            pltpu.VMEM((HALVES, held, rows, quart), bf16),
            pltpu.VMEM((3 * (channels // LANES), (side + 2) * PADDED, LANES), bf16),
            pltpu.VMEM((2, (side + 2) * PADDED, (side + 2) * PADDED), bf16),
            pltpu.VMEM((HALVES, quart, cols), f32),
            pltpu.VMEM((HALVES, quart, cols), f32),
            pltpu.VMEM((HALVES, nd, 2 * per_dp, cols), bf16),
            pltpu.VMEM((HALVES, nd, 2 * per_dp, cols), bf16),
            dma((nh, 2)),
            dma((nh, 2)),
            dma((nh, 2, examples)),
            dma((nh, 2, examples)),
            dma((HALVES, nh, 2, examples)),
            dma((HALVES, nh, 2, examples)),
            dma((HALVES, nd)),
            dma((HALVES, nd)),
        ],
        compiler_params=pltpu.CompilerParams(
            collective_id=0, has_side_effects=True, vmem_limit_bytes=52 * 1024 * 1024
        ),
    )(inputs, out_grads, patch_basis, output_basis)


def solution(mesh):
    in_specs = (
        P(("dp", "fsdp"), None, None, None),
        P(("dp", "fsdp"), None, None, None),
        P(None, "fsdp"),
        P(None, "fsdp"),
    )
    out_specs = (P("dp", "fsdp"), P("dp", "fsdp"))
    return jax.shard_map(
        on_device, mesh=mesh, in_specs=in_specs, out_specs=out_specs, check_vma=False
    )
```

```python
import functools
import math

import jax
import jax.numpy as jnp
from jax import lax
from jax.experimental import pallas as pl
from jax.experimental.pallas import tpu as pltpu
from jax.sharding import PartitionSpec as P

MESH = pl.DeviceIdType.MESH
HALVES = 2
PADDED = 16
LANES = 128


def kernel(
    nd, nf, examples, x_hbm, g_hbm, pb_hbm, ob_hbm, sq_out, ln_out,
    x_ref, g_ref, pb_ref, ob_ref, local,
    xbuf, gstage, obbuf, rot, gr, taps, shifts, sq, ln, rs_send, rs_recv,
    ob_snd, ob_rcv, x_snd, x_rcv, g_snd, g_rcv, r_snd, r_rcv,
):
    d = lax.axis_index("dp")
    f = lax.axis_index("fsdp")
    nh = nf // 2
    h, c = f // 2, f % 2
    sibling = 2 * h + 1 - c
    side = x_ref.shape[1]
    channels = x_ref.shape[3]
    height, cols = pb_ref.shape
    outc = ob_ref.shape[0]
    own_cols = ob_ref.shape[1]
    rows = side * PADDED
    flat = xbuf.shape[1] * PADDED
    quart = outc // HALVES
    per_dp = quart // nd
    total = nd * nf * examples
    f32, bf16 = jnp.float32, jnp.bfloat16

    barrier = pltpu.get_barrier_semaphore()
    pl.semaphore_signal(barrier, inc=1, device_id=(d, sibling), device_id_type=MESH)
    for j in range(1, nh):
        pl.semaphore_signal(
            barrier, inc=1, device_id=(d, 2 * ((h + j) % nh) + c), device_id_type=MESH
        )
    for j in range(1, nd):
        pl.semaphore_signal(barrier, inc=1, device_id=((d + j) % nd, f), device_id_type=MESH)

    def source(j, t):
        return 2 * ((h + j) % nh) + c + t * (1 - 2 * c)

    loads = [
        pltpu.make_async_copy(src, dst, local.at[k])
        for k, (src, dst) in enumerate(
            ((x_hbm, x_ref), (ob_hbm, ob_ref), (g_hbm, g_ref), (pb_hbm, pb_ref))
        )
    ]
    for load in loads:
        load.start()

    def clear(n, carry):
        xbuf[n, 0] = jnp.zeros((PADDED, channels), bf16)
        xbuf[n, pl.ds(side + 1, xbuf.shape[1] - side - 1)] = jnp.zeros(
            (xbuf.shape[1] - side - 1, PADDED, channels), bf16
        )
        return carry

    lax.fori_loop(0, nf * examples, clear, 0)

    def stage(e, carry):
        n = f * examples + e
        xbuf[n, pl.ds(1, side)] = jnp.zeros((side, PADDED, channels), bf16)
        xbuf[n, pl.ds(1, side), pl.ds(0, side), :] = x_ref[e]
        return carry

    loads[0].wait()
    lax.fori_loop(0, examples, stage, 0)
    loads[1].wait()
    obbuf[f] = ob_ref[...]

    pl.semaphore_wait(barrier, nd - 1 + nh)

    def route(j, t):
        to = jnp.where(t == 1, sibling, 2 * ((h + j) % nh) + c)
        back = (nh - j) % nh if isinstance(j, int) else lax.rem(nh - j, nh)
        return (d, to), back

    def ob_copy(j, t, own):
        to, back = route(j, t)
        s = f if own else source(j, 0)
        slot = back if t == 0 else j
        return pltpu.make_async_remote_copy(
            src_ref=obbuf.at[s], dst_ref=obbuf.at[s], send_sem=ob_snd.at[j, t],
            recv_sem=ob_rcv.at[slot, t], device_id=to, device_id_type=MESH)

    def ob_arrival(j, t):
        s = source(j, t)
        return pltpu.make_async_remote_copy(
            src_ref=obbuf.at[s], dst_ref=obbuf.at[s], send_sem=ob_snd.at[j, t],
            recv_sem=ob_rcv.at[j, t], device_id=(d, sibling), device_id_type=MESH)

    def x_copy(j, t, e, own):
        to, back = route(j, t)
        s = f if own else source(j, 0)
        slot = back if t == 0 else j
        ref = xbuf.at[s * examples + e, pl.ds(1, side)]
        return pltpu.make_async_remote_copy(
            src_ref=ref, dst_ref=ref, send_sem=x_snd.at[j, t, e],
            recv_sem=x_rcv.at[slot, t, e], device_id=to, device_id_type=MESH)

    def x_arrival(j, t, e):
        ref = xbuf.at[source(j, t) * examples + e, pl.ds(1, side)]
        return pltpu.make_async_remote_copy(
            src_ref=ref, dst_ref=ref, send_sem=x_snd.at[j, t, e],
            recv_sem=x_rcv.at[j, t, e], device_id=(d, sibling), device_id_type=MESH)

    def g_copy(q, j, t, e, own):
        to, back = route(j, t)
        s = f if own else source(j, 0)
        slot = back if t == 0 else j
        ref = gr.at[q, s * examples + e]
        return pltpu.make_async_remote_copy(
            src_ref=ref, dst_ref=ref, send_sem=g_snd.at[q, j, t, e],
            recv_sem=g_rcv.at[q, slot, t, e], device_id=to, device_id_type=MESH)

    def g_arrival(q, j, t, e):
        ref = gr.at[q, source(j, t) * examples + e]
        return pltpu.make_async_remote_copy(
            src_ref=ref, dst_ref=ref, send_sem=g_snd.at[q, j, t, e],
            recv_sem=g_rcv.at[q, j, t, e], device_id=(d, sibling), device_id_type=MESH)

    def r_copy(q, j):
        return pltpu.make_async_remote_copy(
            src_ref=rs_send.at[q, j], dst_ref=rs_recv.at[q, j], send_sem=r_snd.at[q, j],
            recv_sem=r_rcv.at[q, j], device_id=((d + j) % nd, f), device_id_type=MESH)

    def each(count, body):
        def step(i, carry):
            body(i)
            return carry
        lax.fori_loop(0, count, step, 0)

    for j in range(1, nh):
        ob_copy(j, 0, True).start()
    ob_copy(0, 1, True).start()
    for j in range(1, nh):
        each(examples, lambda e: x_copy(j, 0, e, True).start())
    each(examples, lambda e: x_copy(0, 1, e, True).start())

    sq[...] = jnp.zeros_like(sq)
    ln[...] = jnp.zeros_like(ln)
    into = lax.broadcasted_iota(jnp.int32, (flat, flat), 0)
    out_of = lax.broadcasted_iota(jnp.int32, (flat, flat), 1)
    shifts[0] = (out_of == into - 1).astype(f32).astype(bf16)
    shifts[1] = (out_of == into + 1).astype(f32).astype(bf16)

    chunks = channels // LANES
    first = ((f * cols) // height) * (height // LANES)

    def rotate(slots):
        lines = []
        for b, n in enumerate(slots):
            plain = xbuf[n].reshape(flat, channels)
            before = jnp.dot(shifts[0], plain, preferred_element_type=f32).astype(bf16)
            after = jnp.dot(shifts[1], plain, preferred_element_type=f32).astype(bf16)
            for kx, value in enumerate((before, plain, after)):
                for k in range(chunks):
                    taps[b, kx * chunks + k] = value[:, k * LANES : (k + 1) * LANES]
        for b, n in enumerate(slots):
            pieces = []
            for i in range(height // LANES):
                at = first + i
                tap, k = at // chunks, at % chunks
                ky, kx = tap // 3, tap % 3
                start = pl.multiple_of(ky * PADDED, PADDED)
                pieces.append(taps[b, kx * chunks + k, pl.ds(start, rows), :])
            lines.append(jnp.concatenate(pieces, axis=1))
        patches = jnp.concatenate(lines, axis=0)
        value = jnp.dot(patches, pb_ref[...], preferred_element_type=f32).astype(bf16)
        for b, n in enumerate(slots):
            rot[n] = value[b * rows : (b + 1) * rows]

    def project_whole(n):
        both = jnp.concatenate([gr[q, n] for q in range(HALVES)], axis=1)
        value = lax.dot_general(
            both, rot[n], (((0,), (0,)), ((), ())), preferred_element_type=f32
        ) * (1.0 / side)
        for q in range(HALVES):
            part = value[q * quart : (q + 1) * quart]
            sq[q] += part * part
            ln[q] += part

    def project(q, n):
        value = lax.dot_general(
            gr[q, n], rot[n], (((0,), (0,)), ((), ())), preferred_element_type=f32
        ) * (1.0 / side)
        sq[q] += value * value
        ln[q] += value

    loads[3].wait()
    rotate([f * examples + e for e in range(examples)])

    ob_arrival(0, 1).wait_recv()
    for j in range(1, nh):
        ob_arrival(j, 0).wait_recv()
        ob_copy(j, 1, False).start()
    for j in range(1, nh):
        ob_arrival(j, 1).wait_recv()
    column = lax.broadcasted_iota(jnp.int32, (own_cols, outc), 0)
    place = lax.broadcasted_iota(jnp.int32, (own_cols, outc), 1)
    half, rest = place // quart, place % quart
    wanted = (rest // per_dp) * (per_dp * HALVES) + half * per_dp + rest % per_dp
    basis = jnp.zeros((outc, outc), f32)
    for s in range(nf):
        pick = (column + s * own_cols == wanted).astype(f32).astype(bf16)
        basis = basis + jnp.dot(obbuf[s], pick, preferred_element_type=f32)
    basis = basis.astype(bf16)
    loads[2].wait()
    for e in range(examples):
        gstage[e] = jnp.zeros((side, PADDED, outc), bf16)
        gstage[e, :, pl.ds(0, side), :] = g_ref[e]
        value = jnp.dot(
            gstage[e].reshape(rows, outc), basis, preferred_element_type=f32
        ).astype(bf16)
        for q in range(HALVES):
            gr[q, f * examples + e] = value[:, q * quart : (q + 1) * quart]
    for q in range(HALVES):
        for j in range(1, nh):
            each(examples, lambda e: g_copy(q, j, 0, e, True).start())
        each(examples, lambda e: g_copy(q, 0, 1, e, True).start())

    each(examples, lambda e: project_whole(f * examples + e))

    each(examples, lambda e: x_arrival(0, 1, e).wait_recv())
    rotate([sibling * examples + e for e in range(examples)])

    def sibling_project(e):
        for q in range(HALVES):
            g_arrival(q, 0, 1, e).wait_recv()
        project_whole(sibling * examples + e)

    each(examples, sibling_project)

    def far_rotate(i):
        j, e = 1 + i // examples, i % examples
        x_arrival(j, 0, e).wait_recv()
        x_copy(j, 1, e, False).start()
        x_arrival(j, 1, e).wait_recv()
        rotate([source(j, 0) * examples + e, source(j, 1) * examples + e])

    each((nh - 1) * examples, far_rotate)

    for q in range(HALVES):
        def far_project(i):
            j, e = 1 + i // examples, i % examples
            g_arrival(q, j, 0, e).wait_recv()
            g_copy(q, j, 1, e, False).start()
            project(q, source(j, 0) * examples + e)
            g_arrival(q, j, 1, e).wait_recv()
            project(q, source(j, 1) * examples + e)

        each((nh - 1) * examples, far_project)

        def hand_out(i):
            j = i + 1
            start = pl.multiple_of(((d + j) % nd) * per_dp, per_dp)
            both = jnp.concatenate(
                [sq[q, pl.ds(start, per_dp), :], ln[q, pl.ds(start, per_dp), :]], axis=0
            )
            rs_send[q, j] = both.astype(bf16)
            r_copy(q, j).start()

        each(nd - 1, hand_out)

    for q in range(HALVES):
        start = pl.multiple_of(d * per_dp, per_dp)
        total_sq = sq[q, pl.ds(start, per_dp), :]
        total_ln = ln[q, pl.ds(start, per_dp), :]
        for j in range(1, nd):
            r_copy(q, j).wait_recv()
            got = rs_recv[q, j].astype(f32)
            total_sq = total_sq + got[:per_dp]
            total_ln = total_ln + got[per_dp:]
        sq_out[pl.ds(q * per_dp, per_dp), :] = total_sq * (1.0 / total)
        ln_out[pl.ds(q * per_dp, per_dp), :] = total_ln * (1.0 / math.sqrt(total))

    ob_copy(0, 1, True).wait_send()
    each(examples, lambda e: x_copy(0, 1, e, True).wait_send())
    for q in range(HALVES):
        each(examples, lambda e: g_copy(q, 0, 1, e, True).wait_send())
        each(nd - 1, lambda i: r_copy(q, i + 1).wait_send())
    for j in range(1, nh):
        ob_copy(j, 0, True).wait_send()
        ob_copy(j, 1, False).wait_send()

        def sent(e):
            x_copy(j, 0, e, True).wait_send()
            x_copy(j, 1, e, False).wait_send()
            for q in range(HALVES):
                g_copy(q, j, 0, e, True).wait_send()
                g_copy(q, j, 1, e, False).wait_send()

        each(examples, sent)


def on_device(inputs, out_grads, patch_basis, output_basis):
    nd, nf = lax.axis_size("dp"), lax.axis_size("fsdp")
    nh = nf // 2
    examples, side, _, channels = inputs.shape
    cols = patch_basis.shape[1]
    outc, own_cols = output_basis.shape
    rows = side * PADDED
    quart = outc // HALVES
    per_dp = quart // nd
    held = nf * examples
    bf16, f32 = jnp.bfloat16, jnp.float32
    dma = pltpu.SemaphoreType.DMA
    vmem = pl.BlockSpec(memory_space=pltpu.VMEM)
    out = jax.ShapeDtypeStruct((outc // nd, cols), f32)
    return pl.pallas_call(
        functools.partial(kernel, nd, nf, examples),
        out_shape=(out, out),
        in_specs=[pl.BlockSpec(memory_space=pl.ANY)] * 4,
        out_specs=(vmem, vmem),
        scratch_shapes=[
            pltpu.VMEM(inputs.shape, bf16),
            pltpu.VMEM(out_grads.shape, bf16),
            pltpu.VMEM(patch_basis.shape, bf16),
            pltpu.VMEM(output_basis.shape, bf16),
            dma((4,)),
            pltpu.VMEM((held, side + 2, PADDED, channels), bf16),
            pltpu.VMEM((examples, side, PADDED, outc), bf16),
            pltpu.VMEM((nf, outc, own_cols), bf16),
            pltpu.VMEM((held, rows, cols), bf16),
            pltpu.VMEM((HALVES, held, rows, quart), bf16),
            pltpu.VMEM((examples, 3 * (channels // LANES), (side + 2) * PADDED, LANES), bf16),
            pltpu.VMEM((2, (side + 2) * PADDED, (side + 2) * PADDED), bf16),
            pltpu.VMEM((HALVES, quart, cols), f32),
            pltpu.VMEM((HALVES, quart, cols), f32),
            pltpu.VMEM((HALVES, nd, 2 * per_dp, cols), bf16),
            pltpu.VMEM((HALVES, nd, 2 * per_dp, cols), bf16),
            dma((nh, 2)),
            dma((nh, 2)),
            dma((nh, 2, examples)),
            dma((nh, 2, examples)),
            dma((HALVES, nh, 2, examples)),
            dma((HALVES, nh, 2, examples)),
            dma((HALVES, nd)),
            dma((HALVES, nd)),
        ],
        compiler_params=pltpu.CompilerParams(
            collective_id=0, has_side_effects=True, vmem_limit_bytes=52 * 1024 * 1024
        ),
    )(inputs, out_grads, patch_basis, output_basis)


def solution(mesh):
    in_specs = (
        P(("dp", "fsdp"), None, None, None),
        P(("dp", "fsdp"), None, None, None),
        P(None, "fsdp"),
        P(None, "fsdp"),
    )
    out_specs = (P("dp", "fsdp"), P("dp", "fsdp"))
    return jax.shard_map(
        on_device, mesh=mesh, in_specs=in_specs, out_specs=out_specs, check_vma=False
    )
```

```python
import functools
import math

import jax
import jax.numpy as jnp
from jax import lax
from jax.experimental import pallas as pl
from jax.experimental.pallas import tpu as pltpu
from jax.sharding import PartitionSpec as P

MESH = pl.DeviceIdType.MESH
HALVES = 2
PADDED = 16
LANES = 128


def kernel(
    nd, nf, examples, x_hbm, g_hbm, pb_hbm, ob_hbm, sq_out, ln_out,
    x_ref, g_ref, pb_ref, ob_ref, local, basis_in,
    xbuf, gstage, obbuf, rot, gr, taps, shifts, sq, ln, rs_send, rs_recv,
    ob_snd, ob_rcv, x_snd, x_rcv, g_snd, g_rcv, r_snd, r_rcv,
):
    d = lax.axis_index("dp")
    f = lax.axis_index("fsdp")
    nh = nf // 2
    h, c = f // 2, f % 2
    sibling = 2 * h + 1 - c
    side = x_ref.shape[1]
    channels = x_ref.shape[3]
    cols, height = pb_ref.shape
    own_cols, outc = ob_ref.shape
    rows = side * PADDED
    flat = xbuf.shape[1] * PADDED
    quart = outc // HALVES
    per_dp = quart // nd
    total = nd * nf * examples
    f32, bf16 = jnp.float32, jnp.bfloat16

    barrier = pltpu.get_barrier_semaphore()
    pl.semaphore_signal(barrier, inc=1, device_id=(d, sibling), device_id_type=MESH)
    for j in range(1, nh):
        pl.semaphore_signal(
            barrier, inc=1, device_id=(d, 2 * ((h + j) % nh) + c), device_id_type=MESH
        )
    for j in range(1, nd):
        pl.semaphore_signal(barrier, inc=1, device_id=((d + j) % nd, f), device_id_type=MESH)

    def source(j, t):
        return 2 * ((h + j) % nh) + c + t * (1 - 2 * c)

    loads = [
        pltpu.make_async_copy(src, dst, local.at[k])
        for k, (src, dst) in enumerate(
            ((x_hbm, x_ref), (ob_hbm, ob_ref), (g_hbm, g_ref), (pb_hbm, pb_ref))
        )
    ]
    for load in loads:
        load.start()

    def clear(n, carry):
        xbuf[n, 0] = jnp.zeros((PADDED, channels), bf16)
        xbuf[n, pl.ds(side + 1, xbuf.shape[1] - side - 1)] = jnp.zeros(
            (xbuf.shape[1] - side - 1, PADDED, channels), bf16
        )
        return carry

    lax.fori_loop(0, nf * examples, clear, 0)

    def stage(e, carry):
        n = f * examples + e
        xbuf[n, pl.ds(1, side)] = jnp.zeros((side, PADDED, channels), bf16)
        xbuf[n, pl.ds(1, side), pl.ds(0, side), :] = x_ref[e]
        return carry

    loads[0].wait()
    lax.fori_loop(0, examples, stage, 0)
    loads[1].wait()
    obbuf[f] = ob_ref[...]

    pl.semaphore_wait(barrier, nd - 1 + nh)

    def route(j, t):
        to = jnp.where(t == 1, sibling, 2 * ((h + j) % nh) + c)
        back = (nh - j) % nh if isinstance(j, int) else lax.rem(nh - j, nh)
        return (d, to), back

    def ob_copy(j, t, own):
        to, back = route(j, t)
        s = f if own else source(j, 0)
        slot = back if t == 0 else j
        return pltpu.make_async_remote_copy(
            src_ref=obbuf.at[s], dst_ref=obbuf.at[s], send_sem=ob_snd.at[j, t],
            recv_sem=ob_rcv.at[slot, t], device_id=to, device_id_type=MESH)

    def ob_arrival(j, t):
        s = source(j, t)
        return pltpu.make_async_remote_copy(
            src_ref=obbuf.at[s], dst_ref=obbuf.at[s], send_sem=ob_snd.at[j, t],
            recv_sem=ob_rcv.at[j, t], device_id=(d, sibling), device_id_type=MESH)

    def x_copy(j, t, e, own):
        to, back = route(j, t)
        s = f if own else source(j, 0)
        slot = back if t == 0 else j
        ref = xbuf.at[s * examples + e, pl.ds(1, side)]
        return pltpu.make_async_remote_copy(
            src_ref=ref, dst_ref=ref, send_sem=x_snd.at[j, t, e],
            recv_sem=x_rcv.at[slot, t, e], device_id=to, device_id_type=MESH)

    def x_arrival(j, t, e):
        ref = xbuf.at[source(j, t) * examples + e, pl.ds(1, side)]
        return pltpu.make_async_remote_copy(
            src_ref=ref, dst_ref=ref, send_sem=x_snd.at[j, t, e],
            recv_sem=x_rcv.at[j, t, e], device_id=(d, sibling), device_id_type=MESH)

    def g_copy(q, j, t, e, own):
        to, back = route(j, t)
        s = f if own else source(j, 0)
        slot = back if t == 0 else j
        ref = gr.at[q, s * examples + e]
        return pltpu.make_async_remote_copy(
            src_ref=ref, dst_ref=ref, send_sem=g_snd.at[q, j, t, e],
            recv_sem=g_rcv.at[q, slot, t, e], device_id=to, device_id_type=MESH)

    def g_arrival(q, j, t, e):
        ref = gr.at[q, source(j, t) * examples + e]
        return pltpu.make_async_remote_copy(
            src_ref=ref, dst_ref=ref, send_sem=g_snd.at[q, j, t, e],
            recv_sem=g_rcv.at[q, j, t, e], device_id=(d, sibling), device_id_type=MESH)

    def r_copy(q, j):
        return pltpu.make_async_remote_copy(
            src_ref=rs_send.at[q, j], dst_ref=rs_recv.at[q, j], send_sem=r_snd.at[q, j],
            recv_sem=r_rcv.at[q, j], device_id=((d + j) % nd, f), device_id_type=MESH)

    def each(count, body):
        def step(i, carry):
            body(i)
            return carry
        lax.fori_loop(0, count, step, 0)

    for j in range(1, nh):
        ob_copy(j, 0, True).start()
    ob_copy(0, 1, True).start()
    first_in = examples // 2
    for e in range(first_in):
        for j in range(1, nh):
            x_copy(j, 0, e, True).start()
    each(examples, lambda e: x_copy(0, 1, e, True).start())

    sq[...] = jnp.zeros_like(sq)
    ln[...] = jnp.zeros_like(ln)
    into = lax.broadcasted_iota(jnp.int32, (flat, flat), 0)
    out_of = lax.broadcasted_iota(jnp.int32, (flat, flat), 1)
    shifts[0] = (out_of == into - 1).astype(f32).astype(bf16)
    shifts[1] = (out_of == into + 1).astype(f32).astype(bf16)

    chunks = channels // LANES
    first = ((f * cols) // height) * (height // LANES)

    def rotate(slots):
        lines = []
        for b, n in enumerate(slots):
            plain = xbuf[n].reshape(flat, channels)
            before = jnp.dot(shifts[0], plain, preferred_element_type=f32).astype(bf16)
            after = jnp.dot(shifts[1], plain, preferred_element_type=f32).astype(bf16)
            for kx, value in enumerate((before, plain, after)):
                for k in range(chunks):
                    taps[b, kx * chunks + k] = value[:, k * LANES : (k + 1) * LANES]
        for b, n in enumerate(slots):
            pieces = []
            for i in range(height // LANES):
                at = first + i
                tap, k = at // chunks, at % chunks
                ky, kx = tap // 3, tap % 3
                start = pl.multiple_of(ky * PADDED, PADDED)
                pieces.append(taps[b, kx * chunks + k, pl.ds(start, rows), :])
            lines.append(jnp.concatenate(pieces, axis=1))
        patches = jnp.concatenate(lines, axis=0)
        value = jnp.dot(patches, basis_in[...], preferred_element_type=f32).astype(bf16)
        for b, n in enumerate(slots):
            rot[n] = value[b * rows : (b + 1) * rows]

    def project_whole(n):
        both = jnp.concatenate([gr[q, n] for q in range(HALVES)], axis=1)
        value = lax.dot_general(
            both, rot[n], (((0,), (0,)), ((), ())), preferred_element_type=f32
        ) * (1.0 / side)
        for q in range(HALVES):
            part = value[q * quart : (q + 1) * quart]
            sq[q] += part * part
            ln[q] += part

    def project(q, n):
        value = lax.dot_general(
            gr[q, n], rot[n], (((0,), (0,)), ((), ())), preferred_element_type=f32
        ) * (1.0 / side)
        sq[q] += value * value
        ln[q] += value

    loads[3].wait()
    basis_in[...] = pb_ref[...].T
    rotate([f * examples + e for e in range(examples)])

    ob_arrival(0, 1).wait_recv()
    for j in range(1, nh):
        ob_arrival(j, 0).wait_recv()
        ob_copy(j, 1, False).start()
    for j in range(1, nh):
        ob_arrival(j, 1).wait_recv()
    column = lax.broadcasted_iota(jnp.int32, (outc, outc), 0)
    place = lax.broadcasted_iota(jnp.int32, (outc, outc), 1)
    half, rest = place // quart, place % quart
    wanted = (rest // per_dp) * (per_dp * HALVES) + half * per_dp + rest % per_dp
    pick = (column == wanted).astype(f32).astype(bf16)
    basis = lax.dot_general(
        obbuf[...].reshape(outc, outc), pick, (((0,), (0,)), ((), ())),
        preferred_element_type=f32,
    ).astype(bf16)
    loads[2].wait()
    for e in range(examples):
        gstage[e] = jnp.zeros((side, PADDED, outc), bf16)
        gstage[e, :, pl.ds(0, side), :] = g_ref[e]
        value = jnp.dot(
            gstage[e].reshape(rows, outc), basis, preferred_element_type=f32
        ).astype(bf16)
        for q in range(HALVES):
            gr[q, f * examples + e] = value[:, q * quart : (q + 1) * quart]
    for q in range(HALVES):
        each(examples, lambda e: g_copy(q, 0, 1, e, True).start())

    def send_on(last, following):
        for j in range(1, nh):
            last(j).wait_send()
            for later in following:
                later(j).start()

    for e in range(first_in):
        send_on(
            lambda j: x_copy(j, 0, e, True),
            [lambda j: x_copy(j, 0, e + first_in, True)],
        )
    each(examples, lambda e: project_whole(f * examples + e))

    each(examples, lambda e: x_arrival(0, 1, e).wait_recv())
    rotate([sibling * examples + e for e in range(examples)])

    for e in range(first_in):
        send_on(
            lambda j: x_copy(j, 0, e + first_in, True),
            [
                lambda j: g_copy(0, j, 0, 2 * e, True),
                lambda j: g_copy(0, j, 0, 2 * e + 1, True),
            ],
        )

    def sibling_project(e):
        for q in range(HALVES):
            g_arrival(q, 0, 1, e).wait_recv()
        project_whole(sibling * examples + e)

    def far_rotate(i):
        j, e = 1 + i // examples, i % examples
        x_arrival(j, 0, e).wait_recv()
        x_copy(j, 1, e, False).start()
        x_arrival(j, 1, e).wait_recv()
        rotate([source(j, 0) * examples + e, source(j, 1) * examples + e])

    near = (nh - 1) * examples // 2
    each(near, far_rotate)
    each(examples, sibling_project)
    each((nh - 1) * examples - near, lambda i: far_rotate(i + near))

    for q in range(HALVES):
        def far_project(i):
            j, e = 1 + i // examples, i % examples
            g_arrival(q, j, 0, e).wait_recv()
            g_copy(q, j, 1, e, False).start()
            project(q, source(j, 0) * examples + e)
            g_arrival(q, j, 1, e).wait_recv()
            project(q, source(j, 1) * examples + e)
            if q + 1 < HALVES:
                g_copy(q, j, 0, e, True).wait_send()
                g_copy(q + 1, j, 0, e, True).start()

        each((nh - 1) * examples, far_project)

        def hand_out(i):
            j = i + 1
            start = pl.multiple_of(((d + j) % nd) * per_dp, per_dp)
            both = jnp.concatenate(
                [sq[q, pl.ds(start, per_dp), :], ln[q, pl.ds(start, per_dp), :]], axis=0
            )
            rs_send[q, j] = both.astype(bf16)
            r_copy(q, j).start()

        each(nd - 1, hand_out)

    for q in range(HALVES):
        start = pl.multiple_of(d * per_dp, per_dp)
        total_sq = sq[q, pl.ds(start, per_dp), :]
        total_ln = ln[q, pl.ds(start, per_dp), :]
        for j in range(1, nd):
            r_copy(q, j).wait_recv()
            got = rs_recv[q, j].astype(f32)
            total_sq = total_sq + got[:per_dp]
            total_ln = total_ln + got[per_dp:]
        sq_out[pl.ds(q * per_dp, per_dp), :] = total_sq * (1.0 / total)
        ln_out[pl.ds(q * per_dp, per_dp), :] = total_ln * (1.0 / math.sqrt(total))

    ob_copy(0, 1, True).wait_send()
    each(examples, lambda e: x_copy(0, 1, e, True).wait_send())
    for q in range(HALVES):
        each(examples, lambda e: g_copy(q, 0, 1, e, True).wait_send())
        each(nd - 1, lambda i: r_copy(q, i + 1).wait_send())
    for j in range(1, nh):
        ob_copy(j, 0, True).wait_send()
        ob_copy(j, 1, False).wait_send()

        def sent(e):
            x_copy(j, 1, e, False).wait_send()
            g_copy(HALVES - 1, j, 0, e, True).wait_send()
            for q in range(HALVES):
                g_copy(q, j, 1, e, False).wait_send()

        each(examples, sent)


def on_device(inputs, out_grads, patch_basis, output_basis):
    patch_basis, output_basis = patch_basis.T, output_basis.T
    nd, nf = lax.axis_size("dp"), lax.axis_size("fsdp")
    nh = nf // 2
    examples, side, _, channels = inputs.shape
    cols = patch_basis.shape[0]
    own_cols, outc = output_basis.shape
    rows = side * PADDED
    quart = outc // HALVES
    per_dp = quart // nd
    held = nf * examples
    bf16, f32 = jnp.bfloat16, jnp.float32
    dma = pltpu.SemaphoreType.DMA
    vmem = pl.BlockSpec(memory_space=pltpu.VMEM)
    out = jax.ShapeDtypeStruct((outc // nd, cols), f32)
    return pl.pallas_call(
        functools.partial(kernel, nd, nf, examples),
        out_shape=(out, out),
        in_specs=[pl.BlockSpec(memory_space=pl.ANY)] * 4,
        out_specs=(vmem, vmem),
        scratch_shapes=[
            pltpu.VMEM(inputs.shape, bf16),
            pltpu.VMEM(out_grads.shape, bf16),
            pltpu.VMEM(patch_basis.shape, bf16),
            pltpu.VMEM(output_basis.shape, bf16),
            dma((4,)),
            pltpu.VMEM(patch_basis.shape[::-1], bf16),
            pltpu.VMEM((held, side + 2, PADDED, channels), bf16),
            pltpu.VMEM((examples, side, PADDED, outc), bf16),
            pltpu.VMEM((nf, own_cols, outc), bf16),
            pltpu.VMEM((held, rows, cols), bf16),
            pltpu.VMEM((HALVES, held, rows, quart), bf16),
            pltpu.VMEM((examples, 3 * (channels // LANES), (side + 2) * PADDED, LANES), bf16),
            pltpu.VMEM((2, (side + 2) * PADDED, (side + 2) * PADDED), bf16),
            pltpu.VMEM((HALVES, quart, cols), f32),
            pltpu.VMEM((HALVES, quart, cols), f32),
            pltpu.VMEM((HALVES, nd, 2 * per_dp, cols), bf16),
            pltpu.VMEM((HALVES, nd, 2 * per_dp, cols), bf16),
            dma((nh, 2)),
            dma((nh, 2)),
            dma((nh, 2, examples)),
            dma((nh, 2, examples)),
            dma((HALVES, nh, 2, examples)),
            dma((HALVES, nh, 2, examples)),
            dma((HALVES, nd)),
            dma((HALVES, nd)),
        ],
        compiler_params=pltpu.CompilerParams(
            collective_id=0, has_side_effects=True, vmem_limit_bytes=52 * 1024 * 1024
        ),
    )(inputs, out_grads, patch_basis, output_basis)


def solution(mesh):
    in_specs = (
        P(("dp", "fsdp"), None, None, None),
        P(("dp", "fsdp"), None, None, None),
        P(None, "fsdp"),
        P(None, "fsdp"),
    )
    out_specs = (P("dp", "fsdp"), P("dp", "fsdp"))
    return jax.shard_map(
        on_device, mesh=mesh, in_specs=in_specs, out_specs=out_specs, check_vma=False
    )
```

```python
import functools
import math

import jax
import jax.numpy as jnp
from jax import lax
from jax.experimental import pallas as pl
from jax.experimental.pallas import tpu as pltpu
from jax.sharding import PartitionSpec as P

MESH = pl.DeviceIdType.MESH
HALVES = 2
PADDED = 16
LANES = 128


def kernel(
    nd, nf, examples, x_hbm, g_hbm, pb_hbm, ob_hbm, sq_out, ln_out,
    x_ref, g_ref, pb_ref, ob_ref, local, basis_in,
    xbuf, gstage, obbuf, rot, gr, taps, shifts, sq, ln, rs_send, rs_recv,
    ob_snd, ob_rcv, x_snd, x_rcv, g_snd, g_rcv, r_snd, r_rcv,
):
    d = lax.axis_index("dp")
    f = lax.axis_index("fsdp")
    nh = nf // 2
    h, c = f // 2, f % 2
    sibling = 2 * h + 1 - c
    side = x_ref.shape[1]
    channels = x_ref.shape[3]
    cols, height = pb_ref.shape
    own_cols, outc = ob_ref.shape
    rows = side * PADDED
    flat = xbuf.shape[1] * PADDED
    quart = outc // HALVES
    per_dp = quart // nd
    total = nd * nf * examples
    f32, bf16 = jnp.float32, jnp.bfloat16

    barrier = pltpu.get_barrier_semaphore()
    pl.semaphore_signal(barrier, inc=1, device_id=(d, sibling), device_id_type=MESH)
    for j in range(1, nh):
        pl.semaphore_signal(
            barrier, inc=1, device_id=(d, 2 * ((h + j) % nh) + c), device_id_type=MESH
        )
    for j in range(1, nd):
        pl.semaphore_signal(barrier, inc=1, device_id=((d + j) % nd, f), device_id_type=MESH)

    def source(j, t):
        return 2 * ((h + j) % nh) + c + t * (1 - 2 * c)

    loads = [
        pltpu.make_async_copy(src, dst, local.at[k])
        for k, (src, dst) in enumerate(
            ((x_hbm, x_ref), (ob_hbm, ob_ref), (g_hbm, g_ref), (pb_hbm, pb_ref))
        )
    ]
    for load in loads:
        load.start()

    def clear(n, carry):
        xbuf[n, 0] = jnp.zeros((PADDED, channels), bf16)
        xbuf[n, pl.ds(side + 1, xbuf.shape[1] - side - 1)] = jnp.zeros(
            (xbuf.shape[1] - side - 1, PADDED, channels), bf16
        )
        rot[n, pl.ds(rows, flat - rows), :] = jnp.zeros((flat - rows, cols), bf16)
        for q in range(HALVES):
            gr[q, n, pl.ds(rows, flat - rows), :] = jnp.zeros((flat - rows, quart), bf16)
        return carry

    lax.fori_loop(0, nf * examples, clear, 0)

    def stage(e, carry):
        n = f * examples + e
        xbuf[n, pl.ds(1, side)] = jnp.zeros((side, PADDED, channels), bf16)
        xbuf[n, pl.ds(1, side), pl.ds(0, side), :] = x_ref[e]
        return carry

    loads[0].wait()
    lax.fori_loop(0, examples, stage, 0)
    loads[1].wait()
    obbuf[f] = ob_ref[...]

    pl.semaphore_wait(barrier, nd - 1 + nh)

    def route(j, t):
        to = jnp.where(t == 1, sibling, 2 * ((h + j) % nh) + c)
        back = (nh - j) % nh if isinstance(j, int) else lax.rem(nh - j, nh)
        return (d, to), back

    def ob_copy(j, t, own):
        to, back = route(j, t)
        s = f if own else source(j, 0)
        slot = back if t == 0 else j
        return pltpu.make_async_remote_copy(
            src_ref=obbuf.at[s], dst_ref=obbuf.at[s], send_sem=ob_snd.at[j, t],
            recv_sem=ob_rcv.at[slot, t], device_id=to, device_id_type=MESH)

    def ob_arrival(j, t):
        s = source(j, t)
        return pltpu.make_async_remote_copy(
            src_ref=obbuf.at[s], dst_ref=obbuf.at[s], send_sem=ob_snd.at[j, t],
            recv_sem=ob_rcv.at[j, t], device_id=(d, sibling), device_id_type=MESH)

    def x_copy(j, t, e, own):
        to, back = route(j, t)
        s = f if own else source(j, 0)
        slot = back if t == 0 else j
        ref = xbuf.at[s * examples + e, pl.ds(1, side)]
        return pltpu.make_async_remote_copy(
            src_ref=ref, dst_ref=ref, send_sem=x_snd.at[j, t, e],
            recv_sem=x_rcv.at[slot, t, e], device_id=to, device_id_type=MESH)

    def x_arrival(j, t, e):
        ref = xbuf.at[source(j, t) * examples + e, pl.ds(1, side)]
        return pltpu.make_async_remote_copy(
            src_ref=ref, dst_ref=ref, send_sem=x_snd.at[j, t, e],
            recv_sem=x_rcv.at[j, t, e], device_id=(d, sibling), device_id_type=MESH)

    def g_copy(q, j, t, e, own):
        to, back = route(j, t)
        s = f if own else source(j, 0)
        slot = back if t == 0 else j
        ref = gr.at[q, s * examples + e, pl.ds(0, rows)]
        return pltpu.make_async_remote_copy(
            src_ref=ref, dst_ref=ref, send_sem=g_snd.at[q, j, t, e],
            recv_sem=g_rcv.at[q, slot, t, e], device_id=to, device_id_type=MESH)

    def g_arrival(q, j, t, e):
        ref = gr.at[q, source(j, t) * examples + e, pl.ds(0, rows)]
        return pltpu.make_async_remote_copy(
            src_ref=ref, dst_ref=ref, send_sem=g_snd.at[q, j, t, e],
            recv_sem=g_rcv.at[q, j, t, e], device_id=(d, sibling), device_id_type=MESH)

    def r_copy(q, j):
        return pltpu.make_async_remote_copy(
            src_ref=rs_send.at[q, j], dst_ref=rs_recv.at[q, j], send_sem=r_snd.at[q, j],
            recv_sem=r_rcv.at[q, j], device_id=((d + j) % nd, f), device_id_type=MESH)

    def each(count, body):
        def step(i, carry):
            body(i)
            return carry
        lax.fori_loop(0, count, step, 0)

    for j in range(1, nh):
        ob_copy(j, 0, True).start()
    ob_copy(0, 1, True).start()
    first_in = examples // 2
    for e in range(first_in):
        for j in range(1, nh):
            x_copy(j, 0, e, True).start()
    each(examples, lambda e: x_copy(0, 1, e, True).start())

    sq[...] = jnp.zeros_like(sq)
    ln[...] = jnp.zeros_like(ln)
    into = lax.broadcasted_iota(jnp.int32, (flat, flat), 0)
    out_of = lax.broadcasted_iota(jnp.int32, (flat, flat), 1)
    shifts[0] = (out_of == into - 1).astype(f32).astype(bf16)
    shifts[1] = (out_of == into + 1).astype(f32).astype(bf16)

    chunks = channels // LANES
    first = ((f * cols) // height) * (height // LANES)

    def rotate(slots):
        lines = []
        for b, n in enumerate(slots):
            plain = xbuf[n].reshape(flat, channels)
            before = jnp.dot(shifts[0], plain, preferred_element_type=f32).astype(bf16)
            after = jnp.dot(shifts[1], plain, preferred_element_type=f32).astype(bf16)
            for kx, value in enumerate((before, plain, after)):
                for k in range(chunks):
                    taps[b, kx * chunks + k] = value[:, k * LANES : (k + 1) * LANES]
        for b, n in enumerate(slots):
            pieces = []
            for i in range(height // LANES):
                at = first + i
                tap, k = at // chunks, at % chunks
                ky, kx = tap // 3, tap % 3
                start = pl.multiple_of(ky * PADDED, PADDED)
                pieces.append(taps[b, kx * chunks + k, pl.ds(start, rows), :])
            lines.append(jnp.concatenate(pieces, axis=1))
        patches = jnp.concatenate(lines, axis=0)
        value = jnp.dot(patches, basis_in[...], preferred_element_type=f32).astype(bf16)
        for b, n in enumerate(slots):
            rot[n, pl.ds(0, rows), :] = value[b * rows : (b + 1) * rows]

    def project_whole(n):
        both = jnp.concatenate([gr[q, n] for q in range(HALVES)], axis=1)
        value = lax.dot_general(
            both, rot[n], (((0,), (0,)), ((), ())), preferred_element_type=f32
        ) * (1.0 / side)
        for q in range(HALVES):
            part = value[q * quart : (q + 1) * quart]
            sq[q] += part * part
            ln[q] += part

    def project(q, n):
        value = lax.dot_general(
            gr[q, n], rot[n], (((0,), (0,)), ((), ())), preferred_element_type=f32
        ) * (1.0 / side)
        sq[q] += value * value
        ln[q] += value

    loads[3].wait()
    basis_in[...] = pb_ref[...].T
    def send_on(last, following):
        for j in range(1, nh):
            last(j).wait_send()
            for later in following:
                later(j).start()

    def rotate_gradients():
        ob_arrival(0, 1).wait_recv()
        for j in range(1, nh):
            ob_arrival(j, 0).wait_recv()
            ob_copy(j, 1, False).start()
        for j in range(1, nh):
            ob_arrival(j, 1).wait_recv()
        column = lax.broadcasted_iota(jnp.int32, (outc, outc), 0)
        place = lax.broadcasted_iota(jnp.int32, (outc, outc), 1)
        half, rest = place // quart, place % quart
        wanted = (rest // per_dp) * (per_dp * HALVES) + half * per_dp + rest % per_dp
        pick = (column == wanted).astype(f32).astype(bf16)
        basis = lax.dot_general(
            obbuf[...].reshape(outc, outc), pick, (((0,), (0,)), ((), ())),
            preferred_element_type=f32,
        ).astype(bf16)
        loads[2].wait()

        def one(e):
            gstage[e] = jnp.zeros((side, PADDED, outc), bf16)
            gstage[e, :, pl.ds(0, side), :] = g_ref[e]
            value = jnp.dot(
                gstage[e].reshape(rows, outc), basis, preferred_element_type=f32
            ).astype(bf16)
            for q in range(HALVES):
                gr[q, f * examples + e, pl.ds(0, rows), :] = value[:, q * quart : (q + 1) * quart]
                g_copy(q, 0, 1, e, True).start()

        each(examples, one)
        for e in range(first_in):
            send_on(
                lambda j: x_copy(j, 0, e, True),
                [lambda j: x_copy(j, 0, e + first_in, True)],
            )

    def queue_first_half():
        for e in range(first_in):
            send_on(
                lambda j: x_copy(j, 0, e + first_in, True),
                [
                    lambda j: g_copy(0, j, 0, 2 * e, True),
                    lambda j: g_copy(0, j, 0, 2 * e + 1, True),
                ],
            )

    pairs = examples // 2

    def pair(i):
        @pl.when(i == pairs)
        def _():
            rotate_gradients()

        k = i - examples
        j, e = 1 + jnp.maximum(k, 0) // examples, jnp.maximum(k, 0) % examples

        @pl.when((i >= pairs) & (i < examples))
        def _():
            for b in range(2):
                x_arrival(0, 1, 2 * (i - pairs) + b).wait_recv()

        @pl.when(i == examples)
        def _():
            queue_first_half()

        @pl.when(i >= examples)
        def _():
            x_arrival(j, 0, e).wait_recv()
            x_copy(j, 1, e, False).start()
            x_arrival(j, 1, e).wait_recv()

        near = jnp.where(i < pairs, f * examples + 2 * i, sibling * examples + 2 * (i - pairs))
        n0 = jnp.where(i < examples, near, source(j, 0) * examples + e)
        n1 = jnp.where(i < examples, near + 1, source(j, 1) * examples + e)
        rotate([n0, n1])

        @pl.when((i >= examples) & (i < 2 * examples))
        def _():
            def whole(b):
                item = 2 * k + b
                at = item % examples

                @pl.when(item >= examples)
                def _():
                    for q in range(HALVES):
                        g_arrival(q, 0, 1, at).wait_recv()

                project_whole(jnp.where(item < examples, f, sibling) * examples + at)

            each(2, whole)

    each(examples + (nh - 1) * examples, pair)

    def half_sum(q):
        def far_project(i):
            j, e = 1 + i // examples, i % examples

            def one(t):
                @pl.when(t == 0)
                def _():
                    g_arrival(q, j, 0, e).wait_recv()
                    g_copy(q, j, 1, e, False).start()

                    @pl.when(q + 1 < HALVES)
                    def _():
                        g_copy(q, j, 0, e, True).wait_send()
                        g_copy(q + 1, j, 0, e, True).start()

                @pl.when(t == 1)
                def _():
                    g_arrival(q, j, 1, e).wait_recv()

                project(q, source(j, t) * examples + e)

            each(2, one)

        each((nh - 1) * examples, far_project)

        def hand_out(i):
            j = i + 1
            start = pl.multiple_of(((d + j) % nd) * per_dp, per_dp)
            both = jnp.concatenate(
                [sq[q, pl.ds(start, per_dp), :], ln[q, pl.ds(start, per_dp), :]], axis=0
            )
            rs_send[q, j] = both.astype(bf16)
            r_copy(q, j).start()

        each(nd - 1, hand_out)

    each(HALVES, half_sum)

    for q in range(HALVES):
        start = pl.multiple_of(d * per_dp, per_dp)
        total_sq = sq[q, pl.ds(start, per_dp), :]
        total_ln = ln[q, pl.ds(start, per_dp), :]
        for j in range(1, nd):
            r_copy(q, j).wait_recv()
            got = rs_recv[q, j].astype(f32)
            total_sq = total_sq + got[:per_dp]
            total_ln = total_ln + got[per_dp:]
        sq_out[pl.ds(q * per_dp, per_dp), :] = total_sq * (1.0 / total)
        ln_out[pl.ds(q * per_dp, per_dp), :] = total_ln * (1.0 / math.sqrt(total))

    ob_copy(0, 1, True).wait_send()
    each(examples, lambda e: x_copy(0, 1, e, True).wait_send())
    for q in range(HALVES):
        each(examples, lambda e: g_copy(q, 0, 1, e, True).wait_send())
        each(nd - 1, lambda i: r_copy(q, i + 1).wait_send())
    for j in range(1, nh):
        ob_copy(j, 0, True).wait_send()
        ob_copy(j, 1, False).wait_send()

        def sent(e):
            x_copy(j, 1, e, False).wait_send()
            g_copy(HALVES - 1, j, 0, e, True).wait_send()
            for q in range(HALVES):
                g_copy(q, j, 1, e, False).wait_send()

        each(examples, sent)


def on_device(inputs, out_grads, patch_basis, output_basis):
    patch_basis, output_basis = patch_basis.T, output_basis.T
    nd, nf = lax.axis_size("dp"), lax.axis_size("fsdp")
    nh = nf // 2
    examples, side, _, channels = inputs.shape
    cols = patch_basis.shape[0]
    own_cols, outc = output_basis.shape
    rows = side * PADDED
    quart = outc // HALVES
    per_dp = quart // nd
    held = nf * examples
    bf16, f32 = jnp.bfloat16, jnp.float32
    dma = pltpu.SemaphoreType.DMA
    vmem = pl.BlockSpec(memory_space=pltpu.VMEM)
    out = jax.ShapeDtypeStruct((outc // nd, cols), f32)
    return pl.pallas_call(
        functools.partial(kernel, nd, nf, examples),
        out_shape=(out, out),
        in_specs=[pl.BlockSpec(memory_space=pl.ANY)] * 4,
        out_specs=(vmem, vmem),
        scratch_shapes=[
            pltpu.VMEM(inputs.shape, bf16),
            pltpu.VMEM(out_grads.shape, bf16),
            pltpu.VMEM(patch_basis.shape, bf16),
            pltpu.VMEM(output_basis.shape, bf16),
            dma((4,)),
            pltpu.VMEM(patch_basis.shape[::-1], bf16),
            pltpu.VMEM((held, side + 2, PADDED, channels), bf16),
            pltpu.VMEM((examples, side, PADDED, outc), bf16),
            pltpu.VMEM((nf, own_cols, outc), bf16),
            pltpu.VMEM((held, rows + 2 * PADDED, cols), bf16),
            pltpu.VMEM((HALVES, held, rows + 2 * PADDED, quart), bf16),
            pltpu.VMEM((2, 3 * (channels // LANES), (side + 2) * PADDED, LANES), bf16),
            pltpu.VMEM((2, (side + 2) * PADDED, (side + 2) * PADDED), bf16),
            pltpu.VMEM((HALVES, quart, cols), f32),
            pltpu.VMEM((HALVES, quart, cols), f32),
            pltpu.VMEM((HALVES, nd, 2 * per_dp, cols), bf16),
            pltpu.VMEM((HALVES, nd, 2 * per_dp, cols), bf16),
            dma((nh, 2)),
            dma((nh, 2)),
            dma((nh, 2, examples)),
            dma((nh, 2, examples)),
            dma((HALVES, nh, 2, examples)),
            dma((HALVES, nh, 2, examples)),
            dma((HALVES, nd)),
            dma((HALVES, nd)),
        ],
        compiler_params=pltpu.CompilerParams(
            collective_id=0, has_side_effects=True, vmem_limit_bytes=52 * 1024 * 1024
        ),
    )(inputs, out_grads, patch_basis, output_basis)


def solution(mesh):
    in_specs = (
        P(("dp", "fsdp"), None, None, None),
        P(("dp", "fsdp"), None, None, None),
        P(None, "fsdp"),
        P(None, "fsdp"),
    )
    out_specs = (P("dp", "fsdp"), P("dp", "fsdp"))
    return jax.shard_map(
        on_device, mesh=mesh, in_specs=in_specs, out_specs=out_specs, check_vma=False
    )
```

```python
import functools
import math

import jax
import jax.numpy as jnp
from jax import lax
from jax.experimental import pallas as pl
from jax.experimental.pallas import tpu as pltpu
from jax.sharding import PartitionSpec as P

MESH = pl.DeviceIdType.MESH
HALVES = 2
PADDED = 16
LANES = 128


def kernel(
    nd, nf, examples, x_hbm, g_hbm, pb_hbm, ob_hbm, sq_out, ln_out,
    x_ref, g_ref, pb_ref, ob_ref, local, basis_in,
    xbuf, gstage, obbuf, rot, gr, taps, shifts, sq, ln, rs_send, rs_recv,
    ob_snd, ob_rcv, x_snd, x_rcv, g_snd, g_rcv, r_snd, r_rcv,
):
    d = lax.axis_index("dp")
    f = lax.axis_index("fsdp")
    nh = nf // 2
    h, c = f // 2, f % 2
    sibling = 2 * h + 1 - c
    side = x_ref.shape[1]
    channels = x_ref.shape[3]
    cols, height = pb_ref.shape
    own_cols, outc = ob_ref.shape
    rows = side * PADDED
    flat = xbuf.shape[1] * PADDED
    quart = outc // HALVES
    per_dp = quart // nd
    f32, bf16 = jnp.float32, jnp.bfloat16

    barrier = pltpu.get_barrier_semaphore()
    pl.semaphore_signal(barrier, inc=1, device_id=(d, sibling), device_id_type=MESH)
    for j in range(1, nh):
        pl.semaphore_signal(
            barrier, inc=1, device_id=(d, 2 * ((h + j) % nh) + c), device_id_type=MESH
        )
    for j in range(1, nd):
        pl.semaphore_signal(barrier, inc=1, device_id=((d + j) % nd, f), device_id_type=MESH)

    def source(j, t):
        return 2 * ((h + j) % nh) + c + t * (1 - 2 * c)

    loads = [
        pltpu.make_async_copy(src, dst, local.at[k])
        for k, (src, dst) in enumerate(
            ((x_hbm, x_ref), (ob_hbm, ob_ref), (g_hbm, g_ref), (pb_hbm, pb_ref))
        )
    ]
    for load in loads:
        load.start()

    def clear(n, carry):
        xbuf[n, 0] = jnp.zeros((PADDED, channels), bf16)
        xbuf[n, pl.ds(side + 1, xbuf.shape[1] - side - 1)] = jnp.zeros(
            (xbuf.shape[1] - side - 1, PADDED, channels), bf16
        )
        return carry

    lax.fori_loop(0, nf * examples, clear, 0)

    def stage(e, carry):
        n = f * examples + e
        xbuf[n, pl.ds(1, side)] = jnp.zeros((side, PADDED, channels), bf16)
        xbuf[n, pl.ds(1, side), pl.ds(0, side), :] = x_ref[e]
        return carry

    loads[0].wait()
    lax.fori_loop(0, examples, stage, 0)
    loads[1].wait()
    obbuf[f] = ob_ref[...]

    pl.semaphore_wait(barrier, nd - 1 + nh)

    def route(j, t):
        to = jnp.where(t == 1, sibling, 2 * ((h + j) % nh) + c)
        back = (nh - j) % nh if isinstance(j, int) else lax.rem(nh - j, nh)
        return (d, to), back

    def ob_copy(j, t, own):
        to, back = route(j, t)
        s = f if own else source(j, 0)
        slot = back if t == 0 else j
        return pltpu.make_async_remote_copy(
            src_ref=obbuf.at[s], dst_ref=obbuf.at[s], send_sem=ob_snd.at[j, t],
            recv_sem=ob_rcv.at[slot, t], device_id=to, device_id_type=MESH)

    def ob_arrival(j, t):
        s = source(j, t)
        return pltpu.make_async_remote_copy(
            src_ref=obbuf.at[s], dst_ref=obbuf.at[s], send_sem=ob_snd.at[j, t],
            recv_sem=ob_rcv.at[j, t], device_id=(d, sibling), device_id_type=MESH)

    def x_copy(j, t, e, own):
        to, back = route(j, t)
        s = f if own else source(j, 0)
        slot = back if t == 0 else j
        ref = xbuf.at[s * examples + e, pl.ds(1, side)]
        return pltpu.make_async_remote_copy(
            src_ref=ref, dst_ref=ref, send_sem=x_snd.at[j, t, e],
            recv_sem=x_rcv.at[slot, t, e], device_id=to, device_id_type=MESH)

    def x_arrival(j, t, e):
        ref = xbuf.at[source(j, t) * examples + e, pl.ds(1, side)]
        return pltpu.make_async_remote_copy(
            src_ref=ref, dst_ref=ref, send_sem=x_snd.at[j, t, e],
            recv_sem=x_rcv.at[j, t, e], device_id=(d, sibling), device_id_type=MESH)

    def g_copy(q, j, t, e, own):
        to, back = route(j, t)
        s = f if own else source(j, 0)
        slot = back if t == 0 else j
        ref = gr.at[q, s * examples + e]
        return pltpu.make_async_remote_copy(
            src_ref=ref, dst_ref=ref, send_sem=g_snd.at[q, j, t, e],
            recv_sem=g_rcv.at[q, slot, t, e], device_id=to, device_id_type=MESH)

    def g_arrival(q, j, t, e):
        ref = gr.at[q, source(j, t) * examples + e]
        return pltpu.make_async_remote_copy(
            src_ref=ref, dst_ref=ref, send_sem=g_snd.at[q, j, t, e],
            recv_sem=g_rcv.at[q, j, t, e], device_id=(d, sibling), device_id_type=MESH)

    def r_copy(q, j):
        return pltpu.make_async_remote_copy(
            src_ref=rs_send.at[q, j], dst_ref=rs_recv.at[q, j], send_sem=r_snd.at[q, j],
            recv_sem=r_rcv.at[q, j], device_id=((d + j) % nd, f), device_id_type=MESH)

    def each(count, body):
        def step(i, carry):
            body(i)
            return carry
        lax.fori_loop(0, count, step, 0)

    for j in range(1, nh):
        ob_copy(j, 0, True).start()
    ob_copy(0, 1, True).start()
    for j in range(1, nh):
        each(examples, lambda e: x_copy(j, 0, e, True).start())
    each(examples, lambda e: x_copy(0, 1, e, True).start())

    sq[...] = jnp.zeros_like(sq)
    ln[...] = jnp.zeros_like(ln)
    into = lax.broadcasted_iota(jnp.int32, (flat, flat), 0)
    out_of = lax.broadcasted_iota(jnp.int32, (flat, flat), 1)
    shifts[0] = (out_of == into - 1).astype(f32).astype(bf16)
    shifts[1] = (out_of == into + 1).astype(f32).astype(bf16)

    chunks = channels // LANES
    first = ((f * cols) // height) * (height // LANES)

    def rotate(slots):
        lines = []
        for b, n in enumerate(slots):
            plain = xbuf[n].reshape(flat, channels)
            before = jnp.dot(shifts[0], plain, preferred_element_type=f32).astype(bf16)
            after = jnp.dot(shifts[1], plain, preferred_element_type=f32).astype(bf16)
            for kx, value in enumerate((before, plain, after)):
                for k in range(chunks):
                    taps[b, kx * chunks + k] = value[:, k * LANES : (k + 1) * LANES]
        for b, n in enumerate(slots):
            pieces = []
            for i in range(height // LANES):
                at = first + i
                tap, k = at // chunks, at % chunks
                ky, kx = tap // 3, tap % 3
                start = pl.multiple_of(ky * PADDED, PADDED)
                pieces.append(taps[b, kx * chunks + k, pl.ds(start, rows), :])
            lines.append(jnp.concatenate(pieces, axis=1))
        patches = jnp.concatenate(lines, axis=0)
        value = jnp.dot(patches, basis_in[...], preferred_element_type=f32).astype(bf16)
        for b, n in enumerate(slots):
            rot[n] = value[b * rows : (b + 1) * rows]

    def project_whole(n):
        both = jnp.concatenate([gr[q, n] for q in range(HALVES)], axis=1)
        value = lax.dot_general(
            both, rot[n], (((0,), (0,)), ((), ())), preferred_element_type=f32
        ) * (1.0 / side)
        for q in range(HALVES):
            part = value[q * quart : (q + 1) * quart]
            sq[q] += part * part
            ln[q] += part

    def project(q, n):
        value = lax.dot_general(
            gr[q, n], rot[n], (((0,), (0,)), ((), ())), preferred_element_type=f32
        ) * (1.0 / side)
        sq[q] += value * value
        ln[q] += value

    loads[3].wait()
    basis_in[...] = pb_ref[...].T
    rotate([f * examples + e for e in range(examples)])

    ob_arrival(0, 1).wait_recv()
    for j in range(1, nh):
        ob_arrival(j, 0).wait_recv()
        ob_copy(j, 1, False).start()
    for j in range(1, nh):
        ob_arrival(j, 1).wait_recv()
    column = lax.broadcasted_iota(jnp.int32, (outc, outc), 0)
    place = lax.broadcasted_iota(jnp.int32, (outc, outc), 1)
    half, rest = place // quart, place % quart
    wanted = (rest // per_dp) * (per_dp * HALVES) + half * per_dp + rest % per_dp
    pick = (column == wanted).astype(f32).astype(bf16)
    basis = lax.dot_general(
        obbuf[...].reshape(outc, outc), pick, (((0,), (0,)), ((), ())),
        preferred_element_type=f32,
    ).astype(bf16)
    loads[2].wait()
    for e in range(examples):
        gstage[e] = jnp.zeros((side, PADDED, outc), bf16)
        gstage[e, :, pl.ds(0, side), :] = g_ref[e]
        value = jnp.dot(
            gstage[e].reshape(rows, outc), basis, preferred_element_type=f32
        ).astype(bf16)
        for q in range(HALVES):
            gr[q, f * examples + e] = value[:, q * quart : (q + 1) * quart]
    for j in range(1, nh):
        each(examples, lambda e: g_copy(0, j, 0, e, True).start())
    for q in range(HALVES):
        each(examples, lambda e: g_copy(q, 0, 1, e, True).start())

    each(examples, lambda e: project_whole(f * examples + e))

    each(examples, lambda e: x_arrival(0, 1, e).wait_recv())
    rotate([sibling * examples + e for e in range(examples)])

    def sibling_project(e):
        for q in range(HALVES):
            g_arrival(q, 0, 1, e).wait_recv()
        project_whole(sibling * examples + e)

    def far_rotate(i):
        j, e = 1 + i // examples, i % examples
        x_arrival(j, 0, e).wait_recv()
        x_copy(j, 1, e, False).start()
        x_arrival(j, 1, e).wait_recv()
        rotate([source(j, 0) * examples + e, source(j, 1) * examples + e])

    near = (nh - 1) * examples // 2
    each(near, far_rotate)
    each(examples, sibling_project)
    each((nh - 1) * examples - near, lambda i: far_rotate(i + near))

    for q in range(HALVES):
        def far_project(i):
            j, e = 1 + i // examples, i % examples
            g_arrival(q, j, 0, e).wait_recv()
            g_copy(q, j, 1, e, False).start()
            project(q, source(j, 0) * examples + e)
            g_arrival(q, j, 1, e).wait_recv()
            project(q, source(j, 1) * examples + e)
            if q + 1 < HALVES:
                g_copy(q, j, 0, e, True).wait_send()
                g_copy(q + 1, j, 0, e, True).start()

        each((nh - 1) * examples, far_project)

        def hand_out(i):
            j = i + 1
            start = pl.multiple_of(((d + j) % nd) * per_dp, per_dp)
            both = jnp.concatenate(
                [sq[q, pl.ds(start, per_dp), :], ln[q, pl.ds(start, per_dp), :]], axis=0
            )
            rs_send[q, j] = both.astype(bf16)
            r_copy(q, j).start()

        each(nd - 1, hand_out)

    for q in range(HALVES):
        start = pl.multiple_of(d * per_dp, per_dp)
        total_sq = sq[q, pl.ds(start, per_dp), :]
        total_ln = ln[q, pl.ds(start, per_dp), :]
        for j in range(1, nd):
            r_copy(q, j).wait_recv()
            got = rs_recv[q, j].astype(f32)
            total_sq = total_sq + got[:per_dp]
            total_ln = total_ln + got[per_dp:]
        sq_out[pl.ds(q * per_dp, per_dp), :] = total_sq
        ln_out[pl.ds(q * per_dp, per_dp), :] = total_ln

    ob_copy(0, 1, True).wait_send()
    each(examples, lambda e: x_copy(0, 1, e, True).wait_send())
    for q in range(HALVES):
        each(examples, lambda e: g_copy(q, 0, 1, e, True).wait_send())
        each(nd - 1, lambda i: r_copy(q, i + 1).wait_send())
    for j in range(1, nh):
        ob_copy(j, 0, True).wait_send()
        ob_copy(j, 1, False).wait_send()

        def sent(e):
            x_copy(j, 0, e, True).wait_send()
            x_copy(j, 1, e, False).wait_send()
            g_copy(HALVES - 1, j, 0, e, True).wait_send()
            for q in range(HALVES):
                g_copy(q, j, 1, e, False).wait_send()

        each(examples, sent)


def on_device(inputs, out_grads, patch_basis, output_basis):
    patch_basis, output_basis = patch_basis.T, output_basis.T
    nd, nf = lax.axis_size("dp"), lax.axis_size("fsdp")
    nh = nf // 2
    examples, side, _, channels = inputs.shape
    cols = patch_basis.shape[0]
    own_cols, outc = output_basis.shape
    rows = side * PADDED
    quart = outc // HALVES
    per_dp = quart // nd
    held = nf * examples
    bf16, f32 = jnp.bfloat16, jnp.float32
    dma = pltpu.SemaphoreType.DMA
    vmem = pl.BlockSpec(memory_space=pltpu.VMEM)
    out = jax.ShapeDtypeStruct((outc // nd, cols), f32)
    total = nd * nf * examples
    squares, linear = pl.pallas_call(
        functools.partial(kernel, nd, nf, examples),
        out_shape=(out, out),
        in_specs=[pl.BlockSpec(memory_space=pl.ANY)] * 4,
        out_specs=(vmem, vmem),
        scratch_shapes=[
            pltpu.VMEM(inputs.shape, bf16),
            pltpu.VMEM(out_grads.shape, bf16),
            pltpu.VMEM(patch_basis.shape, bf16),
            pltpu.VMEM(output_basis.shape, bf16),
            dma((4,)),
            pltpu.VMEM(patch_basis.shape[::-1], bf16),
            pltpu.VMEM((held, side + 2, PADDED, channels), bf16),
            pltpu.VMEM((examples, side, PADDED, outc), bf16),
            pltpu.VMEM((nf, own_cols, outc), bf16),
            pltpu.VMEM((held, rows, cols), bf16),
            pltpu.VMEM((HALVES, held, rows, quart), bf16),
            pltpu.VMEM((examples, 3 * (channels // LANES), (side + 2) * PADDED, LANES), bf16),
            pltpu.VMEM((2, (side + 2) * PADDED, (side + 2) * PADDED), bf16),
            pltpu.VMEM((HALVES, quart, cols), f32),
            pltpu.VMEM((HALVES, quart, cols), f32),
            pltpu.VMEM((HALVES, nd, 2 * per_dp, cols), bf16),
            pltpu.VMEM((HALVES, nd, 2 * per_dp, cols), bf16),
            dma((nh, 2)),
            dma((nh, 2)),
            dma((nh, 2, examples)),
            dma((nh, 2, examples)),
            dma((HALVES, nh, 2, examples)),
            dma((HALVES, nh, 2, examples)),
            dma((HALVES, nd)),
            dma((HALVES, nd)),
        ],
        compiler_params=pltpu.CompilerParams(
            collective_id=0, has_side_effects=True, vmem_limit_bytes=52 * 1024 * 1024
        ),
    )(inputs, out_grads, patch_basis, output_basis)
    return squares * (1.0 / total), linear * (1.0 / math.sqrt(total))


def solution(mesh):
    in_specs = (
        P(("dp", "fsdp"), None, None, None),
        P(("dp", "fsdp"), None, None, None),
        P(None, "fsdp"),
        P(None, "fsdp"),
    )
    out_specs = (P("dp", "fsdp"), P("dp", "fsdp"))
    return jax.shard_map(
        on_device, mesh=mesh, in_specs=in_specs, out_specs=out_specs, check_vma=False
    )
```

```python
import functools
import math

import jax
import jax.numpy as jnp
from jax import lax
from jax.experimental import pallas as pl
from jax.experimental.pallas import tpu as pltpu
from jax.sharding import PartitionSpec as P

MESH = pl.DeviceIdType.MESH
HALVES = 2
PADDED = 16
LANES = 128


def kernel(
    nd, nf, examples, x_hbm, g_hbm, pb_hbm, ob_hbm, sq_out, ln_out,
    x_ref, g_ref, pb_ref, ob_ref, local, basis_in,
    xbuf, gstage, obbuf, rot, gr, taps, shifts, sq, ln, rs_send, rs_recv,
    ob_snd, ob_rcv, x_snd, x_rcv, g_snd, g_rcv, r_snd, r_rcv,
):
    d = lax.axis_index("dp")
    f = lax.axis_index("fsdp")
    nh = nf // 2
    h, c = f // 2, f % 2
    sibling = 2 * h + 1 - c
    side = x_ref.shape[1]
    channels = x_ref.shape[3]
    cols, height = pb_ref.shape
    own_cols, outc = ob_ref.shape
    rows = side * PADDED
    flat = xbuf.shape[1] * PADDED
    quart = outc // HALVES
    per_dp = quart // nd
    f32, bf16 = jnp.float32, jnp.bfloat16

    barrier = pltpu.get_barrier_semaphore()
    pl.semaphore_signal(barrier, inc=1, device_id=(d, sibling), device_id_type=MESH)
    for j in range(1, nh):
        pl.semaphore_signal(
            barrier, inc=1, device_id=(d, 2 * ((h + j) % nh) + c), device_id_type=MESH
        )
    for j in range(1, nd):
        pl.semaphore_signal(barrier, inc=1, device_id=((d + j) % nd, f), device_id_type=MESH)

    def source(j, t):
        return 2 * ((h + j) % nh) + c + t * (1 - 2 * c)

    loads = [
        pltpu.make_async_copy(src, dst, local.at[k])
        for k, (src, dst) in enumerate(
            ((x_hbm, x_ref), (ob_hbm, ob_ref), (g_hbm, g_ref), (pb_hbm, pb_ref))
        )
    ]
    for load in loads:
        load.start()

    def clear(n, carry):
        xbuf[n, 0] = jnp.zeros((PADDED, channels), bf16)
        xbuf[n, pl.ds(side + 1, xbuf.shape[1] - side - 1)] = jnp.zeros(
            (xbuf.shape[1] - side - 1, PADDED, channels), bf16
        )
        return carry

    lax.fori_loop(0, nf * examples, clear, 0)

    def stage(e, carry):
        n = f * examples + e
        xbuf[n, pl.ds(1, side)] = jnp.zeros((side, PADDED, channels), bf16)
        xbuf[n, pl.ds(1, side), pl.ds(0, side), :] = x_ref[e]
        return carry

    loads[0].wait()
    lax.fori_loop(0, examples, stage, 0)
    loads[1].wait()
    obbuf[f] = ob_ref[...]

    pl.semaphore_wait(barrier, nd - 1 + nh)

    def route(j, t):
        to = jnp.where(t == 1, sibling, 2 * ((h + j) % nh) + c)
        back = (nh - j) % nh if isinstance(j, int) else lax.rem(nh - j, nh)
        return (d, to), back

    def ob_copy(j, t, own):
        to, back = route(j, t)
        s = f if own else source(j, 0)
        slot = back if t == 0 else j
        return pltpu.make_async_remote_copy(
            src_ref=obbuf.at[s], dst_ref=obbuf.at[s], send_sem=ob_snd.at[j, t],
            recv_sem=ob_rcv.at[slot, t], device_id=to, device_id_type=MESH)

    def ob_arrival(j, t):
        s = source(j, t)
        return pltpu.make_async_remote_copy(
            src_ref=obbuf.at[s], dst_ref=obbuf.at[s], send_sem=ob_snd.at[j, t],
            recv_sem=ob_rcv.at[j, t], device_id=(d, sibling), device_id_type=MESH)

    def x_copy(j, t, e, own):
        to, back = route(j, t)
        s = f if own else source(j, 0)
        slot = back if t == 0 else j
        ref = xbuf.at[s * examples + e, pl.ds(1, side)]
        return pltpu.make_async_remote_copy(
            src_ref=ref, dst_ref=ref, send_sem=x_snd.at[j, t, e],
            recv_sem=x_rcv.at[slot, t, e], device_id=to, device_id_type=MESH)

    def x_arrival(j, t, e):
        ref = xbuf.at[source(j, t) * examples + e, pl.ds(1, side)]
        return pltpu.make_async_remote_copy(
            src_ref=ref, dst_ref=ref, send_sem=x_snd.at[j, t, e],
            recv_sem=x_rcv.at[j, t, e], device_id=(d, sibling), device_id_type=MESH)

    def g_copy(q, j, t, e, own):
        to, back = route(j, t)
        s = f if own else source(j, 0)
        slot = back if t == 0 else j
        ref = gr.at[q, s * examples + e]
        return pltpu.make_async_remote_copy(
            src_ref=ref, dst_ref=ref, send_sem=g_snd.at[q, j, t, e],
            recv_sem=g_rcv.at[q, slot, t, e], device_id=to, device_id_type=MESH)

    def g_arrival(q, j, t, e):
        ref = gr.at[q, source(j, t) * examples + e]
        return pltpu.make_async_remote_copy(
            src_ref=ref, dst_ref=ref, send_sem=g_snd.at[q, j, t, e],
            recv_sem=g_rcv.at[q, j, t, e], device_id=(d, sibling), device_id_type=MESH)

    def r_copy(q, j):
        return pltpu.make_async_remote_copy(
            src_ref=rs_send.at[q, j], dst_ref=rs_recv.at[q, j], send_sem=r_snd.at[q, j],
            recv_sem=r_rcv.at[q, j], device_id=((d + j) % nd, f), device_id_type=MESH)

    def each(count, body):
        def step(i, carry):
            body(i)
            return carry
        lax.fori_loop(0, count, step, 0)

    for j in range(1, nh):
        ob_copy(j, 0, True).start()
    ob_copy(0, 1, True).start()
    for j in range(1, nh):
        each(examples, lambda e: x_copy(j, 0, e, True).start())
    each(examples, lambda e: x_copy(0, 1, e, True).start())

    sq[...] = jnp.zeros_like(sq)
    ln[...] = jnp.zeros_like(ln)
    into = lax.broadcasted_iota(jnp.int32, (flat, flat), 0)
    out_of = lax.broadcasted_iota(jnp.int32, (flat, flat), 1)
    shifts[0] = (out_of == into - 1).astype(f32).astype(bf16)
    shifts[1] = (out_of == into + 1).astype(f32).astype(bf16)

    chunks = channels // LANES
    first = ((f * cols) // height) * (height // LANES)

    def rotate(slots):
        lines = []
        for b, n in enumerate(slots):
            plain = xbuf[n].reshape(flat, channels)
            before = jnp.dot(shifts[0], plain, preferred_element_type=f32).astype(bf16)
            after = jnp.dot(shifts[1], plain, preferred_element_type=f32).astype(bf16)
            for kx, value in enumerate((before, plain, after)):
                for k in range(chunks):
                    taps[b, kx * chunks + k] = value[:, k * LANES : (k + 1) * LANES]
        for b, n in enumerate(slots):
            pieces = []
            for i in range(height // LANES):
                at = first + i
                tap, k = at // chunks, at % chunks
                ky, kx = tap // 3, tap % 3
                start = pl.multiple_of(ky * PADDED, PADDED)
                pieces.append(taps[b, kx * chunks + k, pl.ds(start, rows), :])
            lines.append(jnp.concatenate(pieces, axis=1))
        patches = jnp.concatenate(lines, axis=0)
        value = jnp.dot(patches, basis_in[...], preferred_element_type=f32).astype(bf16)
        for b, n in enumerate(slots):
            rot[n] = value[b * rows : (b + 1) * rows]

    def project_whole(n):
        both = jnp.concatenate([gr[q, n] for q in range(HALVES)], axis=1)
        value = lax.dot_general(
            both, rot[n], (((0,), (0,)), ((), ())), preferred_element_type=f32
        ) * (1.0 / side)
        for q in range(HALVES):
            part = value[q * quart : (q + 1) * quart]
            sq[q] += part * part
            ln[q] += part

    def project(q, n):
        value = lax.dot_general(
            gr[q, n], rot[n], (((0,), (0,)), ((), ())), preferred_element_type=f32
        ) * (1.0 / side)
        sq[q] += value * value
        ln[q] += value

    loads[3].wait()
    basis_in[...] = pb_ref[...].T
    rotate([f * examples + e for e in range(examples)])

    ob_arrival(0, 1).wait_recv()
    for j in range(1, nh):
        ob_arrival(j, 0).wait_recv()
        ob_copy(j, 1, False).start()
    for j in range(1, nh):
        ob_arrival(j, 1).wait_recv()
    column = lax.broadcasted_iota(jnp.int32, (outc, outc), 0)
    place = lax.broadcasted_iota(jnp.int32, (outc, outc), 1)
    half, rest = place // quart, place % quart
    wanted = (rest // per_dp) * (per_dp * HALVES) + half * per_dp + rest % per_dp
    pick = (column == wanted).astype(f32).astype(bf16)
    basis = lax.dot_general(
        obbuf[...].reshape(outc, outc), pick, (((0,), (0,)), ((), ())),
        preferred_element_type=f32,
    ).astype(bf16)
    loads[2].wait()
    for e in range(examples):
        gstage[e] = jnp.zeros((side, PADDED, outc), bf16)
        gstage[e, :, pl.ds(0, side), :] = g_ref[e]
        value = jnp.dot(
            gstage[e].reshape(rows, outc), basis, preferred_element_type=f32
        ).astype(bf16)
        for q in range(HALVES):
            gr[q, f * examples + e] = value[:, q * quart : (q + 1) * quart]
    for q in range(HALVES):
        for j in range(1, nh):
            each(examples, lambda e: g_copy(q, j, 0, e, True).start())
        each(examples, lambda e: g_copy(q, 0, 1, e, True).start())

    each(examples, lambda e: project_whole(f * examples + e))

    each(examples, lambda e: x_arrival(0, 1, e).wait_recv())
    rotate([sibling * examples + e for e in range(examples)])

    def sibling_project(e):
        for q in range(HALVES):
            g_arrival(q, 0, 1, e).wait_recv()
        project_whole(sibling * examples + e)

    def far_rotate(i):
        j, e = 1 + i // examples, i % examples
        x_arrival(j, 0, e).wait_recv()
        x_copy(j, 1, e, False).start()
        x_arrival(j, 1, e).wait_recv()
        rotate([source(j, 0) * examples + e, source(j, 1) * examples + e])

    near = (nh - 1) * examples // 2
    each(near, far_rotate)
    each(examples, sibling_project)
    each((nh - 1) * examples - near, lambda i: far_rotate(i + near))

    for q in range(HALVES):
        def far_project(i):
            j, e = 1 + i // examples, i % examples
            g_arrival(q, j, 0, e).wait_recv()
            g_copy(q, j, 1, e, False).start()
            project(q, source(j, 0) * examples + e)
            g_arrival(q, j, 1, e).wait_recv()
            project(q, source(j, 1) * examples + e)

        each((nh - 1) * examples, far_project)

        def hand_out(i):
            j = i + 1
            start = pl.multiple_of(((d + j) % nd) * per_dp, per_dp)
            both = jnp.concatenate(
                [sq[q, pl.ds(start, per_dp), :], ln[q, pl.ds(start, per_dp), :]], axis=0
            )
            rs_send[q, j] = both.astype(bf16)
            r_copy(q, j).start()

        each(nd - 1, hand_out)

    for q in range(HALVES):
        start = pl.multiple_of(d * per_dp, per_dp)
        total_sq = sq[q, pl.ds(start, per_dp), :]
        total_ln = ln[q, pl.ds(start, per_dp), :]
        for j in range(1, nd):
            r_copy(q, j).wait_recv()
            got = rs_recv[q, j].astype(f32)
            total_sq = total_sq + got[:per_dp]
            total_ln = total_ln + got[per_dp:]
        sq_out[pl.ds(q * per_dp, per_dp), :] = total_sq
        ln_out[pl.ds(q * per_dp, per_dp), :] = total_ln

    ob_copy(0, 1, True).wait_send()
    each(examples, lambda e: x_copy(0, 1, e, True).wait_send())
    for q in range(HALVES):
        each(examples, lambda e: g_copy(q, 0, 1, e, True).wait_send())
        each(nd - 1, lambda i: r_copy(q, i + 1).wait_send())
    for j in range(1, nh):
        ob_copy(j, 0, True).wait_send()
        ob_copy(j, 1, False).wait_send()

        def sent(e):
            x_copy(j, 0, e, True).wait_send()
            x_copy(j, 1, e, False).wait_send()
            for q in range(HALVES):
                g_copy(q, j, 0, e, True).wait_send()
                g_copy(q, j, 1, e, False).wait_send()

        each(examples, sent)


def on_device(inputs, out_grads, patch_basis, output_basis):
    patch_basis, output_basis = patch_basis.T, output_basis.T
    nd, nf = lax.axis_size("dp"), lax.axis_size("fsdp")
    nh = nf // 2
    examples, side, _, channels = inputs.shape
    cols = patch_basis.shape[0]
    own_cols, outc = output_basis.shape
    rows = side * PADDED
    quart = outc // HALVES
    per_dp = quart // nd
    held = nf * examples
    bf16, f32 = jnp.bfloat16, jnp.float32
    dma = pltpu.SemaphoreType.DMA
    vmem = pl.BlockSpec(memory_space=pltpu.VMEM)
    out = jax.ShapeDtypeStruct((outc // nd, cols), f32)
    total = nd * nf * examples
    squares, linear = pl.pallas_call(
        functools.partial(kernel, nd, nf, examples),
        out_shape=(out, out),
        in_specs=[pl.BlockSpec(memory_space=pl.ANY)] * 4,
        out_specs=(vmem, vmem),
        scratch_shapes=[
            pltpu.VMEM(inputs.shape, bf16),
            pltpu.VMEM(out_grads.shape, bf16),
            pltpu.VMEM(patch_basis.shape, bf16),
            pltpu.VMEM(output_basis.shape, bf16),
            dma((4,)),
            pltpu.VMEM(patch_basis.shape[::-1], bf16),
            pltpu.VMEM((held, side + 2, PADDED, channels), bf16),
            pltpu.VMEM((examples, side, PADDED, outc), bf16),
            pltpu.VMEM((nf, own_cols, outc), bf16),
            pltpu.VMEM((held, rows, cols), bf16),
            pltpu.VMEM((HALVES, held, rows, quart), bf16),
            pltpu.VMEM((examples, 3 * (channels // LANES), (side + 2) * PADDED, LANES), bf16),
            pltpu.VMEM((2, (side + 2) * PADDED, (side + 2) * PADDED), bf16),
            pltpu.VMEM((HALVES, quart, cols), f32),
            pltpu.VMEM((HALVES, quart, cols), f32),
            pltpu.VMEM((HALVES, nd, 2 * per_dp, cols), bf16),
            pltpu.VMEM((HALVES, nd, 2 * per_dp, cols), bf16),
            dma((nh, 2)),
            dma((nh, 2)),
            dma((nh, 2, examples)),
            dma((nh, 2, examples)),
            dma((HALVES, nh, 2, examples)),
            dma((HALVES, nh, 2, examples)),
            dma((HALVES, nd)),
            dma((HALVES, nd)),
        ],
        compiler_params=pltpu.CompilerParams(
            collective_id=0, has_side_effects=True, vmem_limit_bytes=52 * 1024 * 1024
        ),
    )(inputs, out_grads, patch_basis, output_basis)
    return squares * (1.0 / total), linear * (1.0 / math.sqrt(total))


def solution(mesh):
    in_specs = (
        P(("dp", "fsdp"), None, None, None),
        P(("dp", "fsdp"), None, None, None),
        P(None, "fsdp"),
        P(None, "fsdp"),
    )
    out_specs = (P("dp", "fsdp"), P("dp", "fsdp"))
    return jax.shard_map(
        on_device, mesh=mesh, in_specs=in_specs, out_specs=out_specs, check_vma=False
    )
```
